512 devices in a mesh: expert: 64 (over x, z_lo, y), tensor: 8 (over z_hi, core).
Axes of the slice: x: 4, y: 8, z: 8 (z_hi: 4, z_lo: 2; z = z_hi * 2 + z_lo), core: 2. Of those that a mesh axis runs over, the one named last changes fastest.
Arguments:
- tokens: bfloat16 [16384, 3584], P('expert', 'tensor'), may hold values from -6 to 6
- expert_ids: int32 [16384, 2], P('expert'), may hold values from 0 to 63, all different within a row; in each aligned block of 256 rows (0 to 255, 256 to 511, ...) at most 12 rows name the same one
- weights: bfloat16 [64, 3584, 2, 2432], P('expert', None, None, 'tensor'), may hold values from -0.09375 to 0.09375
Outputs:
- hidden: bfloat16 [16384, 2, 2432], P('expert', None, 'tensor')
The draws below stay inside these ranges and needn't reach their ends.
Inputs may be any that keep to these rules, and one draw needn't show every extreme that they name: `expert_ids`: the two experts of a token differ. Among the 256 tokens of one index of expert, at most 12 name any one expert, and that bound is reached.
All inputs are finite; a program needn't handle non-finite values.
Results may differ from the reference program's by a relative error of at most 0.0013.
Values may be sent and summed in bfloat16 or wider, within the bound.
A program may use at most 64 MiB of HBM per device.

```python
import math
import jax
import jax.numpy as jnp
import numpy as np
from jax import lax

DW = 3584
FFW = 2432
TOK_DEV = 256
EXPERTS = 64
CAP = 12
TOKENS = 16384
N_EXPERT = 64


def block_levels(stream_key, dims, pieces, least, high):
    gain, own = 1.0, jax.random.fold_in(stream_key, 6)
    for dim, shards_of in pieces:
        steps = jnp.exp(jax.random.uniform(jax.random.fold_in(own, dim), (shards_of,), jnp.float32, least / len(pieces), high / len(pieces)))
        gain = gain * jnp.repeat(steps, dims[dim] // shards_of).reshape([-1 if axis == dim else 1 for axis in range(len(dims))])
    return gain


def shared_out(key, own, number, rows, number_of, top, reach, skew):
    ranking = jax.random.permutation(key, number_of)
    crowded, common = portions_of(number_of, rows * top, reach, skew, True), portions_of(number_of, rows * top, reach, skew, False)
    places = jnp.arange(number_of)

    def named(lengths, turn):
        used = int((lengths > 0).sum())
        fixed = max(1, used // 4)
        shifted = fixed + (places - fixed + turn * (used - fixed)) % max(1, number_of - fixed)
        return jnp.zeros((number_of,), jnp.int32).at[ranking[jnp.where(places < fixed, places, shifted)]].set(jnp.asarray(lengths, jnp.int32))

    lengths = jnp.where(number % 4 == 0, named(crowded, number // 4), named(common, number - number // 4 - 1))
    mixed = jax.random.permutation(jax.random.fold_in(own, 3), number_of)
    source_of, taker = mixed[0:number_of // 2 * 2:2], mixed[1:number_of // 2 * 2:2]
    slack = jnp.minimum(lengths[source_of] - 1, reach - lengths[taker]) // 2
    slack = jnp.where((source_of == ranking[0]) | (taker == ranking[0]) | (lengths[taker] == 0), 0, jnp.maximum(slack, 0))
    shifted = jax.random.randint(jax.random.fold_in(own, 4), (number_of // 2,), 0, 1 << 20) % (slack + 1)
    lengths = lengths.at[source_of].add(-shifted).at[taker].add(shifted)
    items = jnp.searchsorted(jnp.cumsum(lengths), jnp.arange(rows * top), side="right").astype(jnp.int32)
    table = items.reshape(top, rows).T
    table = table[jax.random.permutation(jax.random.fold_in(own, 1), rows)]
    turn = jax.random.randint(jax.random.fold_in(own, 2), (rows, 1), 0, top)
    return jnp.take_along_axis(table, (jnp.arange(top)[None, :] + turn) % top, axis=1)


def portions_of(number_of, total, most, slope, full):
    loads = [(1 << 20) // math.isqrt(rank ** slope) + 1 for rank in range(1, number_of + 1)]
    largest = most if full else min(most, max(-(-total // number_of), total * loads[0] // sum(loads)))
    least = 1 if total - largest >= number_of - 1 else 0
    given, surplus = [largest] + [least] * (number_of - 1), total - largest - least * (number_of - 1)
    while surplus > 0:
        free = [i for i in range(1, number_of) if given[i] < largest] or [i for i in range(1, number_of) if given[i] < most]
        mass, remaining = sum([loads[i] for i in free]), surplus
        for i in free:
            addition = min(most - given[i], max(1, remaining * loads[i] // mass), surplus)
            given[i] = given[i] + addition
            surplus = surplus - addition
    return np.array(given)


def centred(rng, shape, width, bound, pieces=(), kind=jnp.bfloat16):
    array = jax.random.normal(rng, shape, jnp.float32) * width
    if len(pieces) > 0:
        array = block_levels(rng, shape, pieces, -0.22, 0.18) * array
    return jnp.clip(array, min=-bound, max=bound).astype(kind)


def setup_inputs(seed: int = 0) -> dict:
    keys = jax.random.split(jax.random.key(seed), 4)
    tokens = centred(keys[0], (TOKENS, DW), 1.0, 6.0, ((0, 64), (1, 8)))
    expert_ids_keys = jax.random.split(jax.random.fold_in(keys[1], 1), TOKENS // TOK_DEV)
    expert_ids_turns = jax.random.permutation(jax.random.fold_in(keys[1], 3), TOKENS // TOK_DEV)
    expert_ids = jax.vmap(lambda own, number: shared_out(jax.random.fold_in(keys[1], 2), own, number, TOK_DEV, EXPERTS, 2, CAP, 2))(expert_ids_keys, expert_ids_turns).reshape((TOKENS, 2))
    weights = centred(keys[2], (EXPERTS, DW, 2, FFW), DW ** -0.5, 0.09375, ((0, 64), (3, 8)))
    return dict(tokens=tokens, expert_ids=expert_ids, weights=weights)


def reference(tokens, expert_ids, weights):
    groups = N_EXPERT
    capacity = CAP
    ids = expert_ids.reshape(groups, TOK_DEV * 2)
    onehot = (ids[:, :, None] == jnp.arange(EXPERTS, dtype=jnp.int32)[None, None, :]).astype(jnp.int32)
    before = jnp.cumsum(onehot, axis=1) - onehot
    position = jnp.sum(before * onehot, axis=2).astype(jnp.int32)
    source = jnp.arange(groups, dtype=jnp.int32)[:, None]
    index = ((ids * groups + source) * capacity + position).reshape(-1).astype(jnp.int32)
    token_index = (jnp.arange(TOKENS * 2, dtype=jnp.int32) // 2).astype(jnp.int32)
    buffer = jnp.zeros((EXPERTS * groups * capacity, DW), tokens.dtype)
    buffer = buffer.at[index].set(tokens[token_index])
    buffer = buffer.reshape(EXPERTS, groups * capacity, DW)

    def one_expert(pair):
        rows, weight = pair
        gate = jnp.dot(rows, weight[:, 0, :], preferred_element_type=jnp.float32)
        up = jnp.dot(rows, weight[:, 1, :], preferred_element_type=jnp.float32)
        return (jax.nn.silu(gate) * up).astype(jnp.bfloat16)

    results = lax.map(one_expert, (buffer, weights))
    flat = results.reshape(EXPERTS * groups * capacity, FFW)
    return flat[index].reshape(TOKENS, 2, FFW)
```

```python
import functools

import jax
import jax.numpy as jnp
from jax import lax
from jax.experimental import pallas as pl
from jax.experimental.pallas import tpu as pltpu
from jax.sharding import PartitionSpec as P

MESH = pl.DeviceIdType.MESH
BF = jnp.bfloat16
F32 = jnp.float32

GROUPS = 3
LANES = 896
HALF = 448
WIDTH = 304
RET = 640
OUTW = 384
UNITS = [(0, 0, 384), (0, 384, 512), (1, 0, 384), (1, 384, 512), (2, 0, 512), (2, 512, 384)]
LAST = {0: 1, 1: 3, 2: 5}


def dot(a, b, dims):
    return lax.dot_general(a, b, (dims, ((), ())), preferred_element_type=F32)


def kernel(
    ids_ref, tok_ref, w_ref, out_ref,
    tokt, ww, ysend, yrecv, xsend, fs, xf, acc, hb, rx, rys, ry, rd, gmap, oacc,
    tsem, wsem, csem, ysem, xsem, zsend, zrecv, r1sem, r2sem, r3sem,
):
    e = lax.axis_index("expert")
    t = lax.axis_index("tensor")
    y = lax.rem(e, 8)
    q = e // 8
    x = q // 2
    zl = lax.rem(q, 2)
    h = t // 2
    c = lax.rem(t, 2)

    def dev(x_, zl_, y_, h_):
        return ((x_ * 2 + zl_) * 8 + y_, h_ * 2 + c)

    other = (e, h * 2 + 1 - c)
    zp1 = dev(x, 1 - zl, y, lax.rem(h + zl, 4))
    zm1 = dev(x, 1 - zl, y, lax.rem(h + zl + 3, 4))
    zp2 = dev(x, zl, y, lax.rem(h + 1, 4))
    zm2 = dev(x, zl, y, lax.rem(h + 3, 4))
    ypeers = [(lax.rem(y + d, 8), dev(x, zl, lax.rem(y + d, 8), h)) for d in (4, 3, 5, 2, 6, 1, 7)]
    xpeers = [(lax.rem(x + d, 4), dev(lax.rem(x + d, 4), zl, y, h)) for d in (2, 1, 3)]
    qpeers = [
        (lax.rem(x + d, 4), f, dev(lax.rem(x + d, 4), (1 - zl) if f else zl, y, h))
        for d, f in ((2, 1), (1, 1), (3, 1), (2, 0), (1, 0), (3, 0), (0, 1))
    ]

    barrier = pltpu.get_barrier_semaphore()
    peers = [p for _, p in ypeers] + [p for _, _, p in qpeers] + [zp1, zm1, zp2, zm2, other]
    for p in peers:
        pl.semaphore_signal(barrier, inc=1, device_id=p, device_id_type=MESH)

    def remote(src, dst, ss, rs, p):
        return pltpu.make_async_remote_copy(
            src_ref=src, dst_ref=dst, send_sem=ss, recv_sem=rs, device_id=p, device_id_type=MESH
        )

    mine = pl.ds(pl.multiple_of(c * HALF, 16), HALF)
    theirs = pl.ds(pl.multiple_of((1 - c) * HALF, 16), HALF)
    tok_local = pltpu.make_async_copy(tok_ref, tokt.at[mine], tsem.at[0])
    tok_local.start()
    w_local = pltpu.make_async_copy(w_ref, ww.at[c], wsem.at[0])
    w_local.start()

    experts = lax.broadcasted_iota(jnp.int32, (64, 256), 0)
    upper = (
        lax.broadcasted_iota(jnp.int32, (256, 256), 0) < lax.broadcasted_iota(jnp.int32, (256, 256), 1)
    ).astype(F32).astype(BF)
    counted = jnp.zeros((64, 1), F32)
    slots = []
    for k in range(2):
        expert = ids_ref[k : k + 1, :]
        hot = (experts == expert).astype(F32)
        before = dot(hot.astype(BF), upper, ((1,), (0,))) + counted
        counted = counted + jnp.sum(hot, axis=1, keepdims=True)
        rank = jnp.sum(before * hot, axis=0, keepdims=True).astype(jnp.int32)
        ey, eq = expert & 7, expert >> 3
        flip = (eq + zl) & 1
        row = ey * 16 + (eq >> 1) * 4 + flip * 2 + ((rank >> 1) & 1)
        slots.append(((rank & 1) * GROUPS + (rank >> 2)) * 128 + row)
    rows_iota = lax.broadcasted_iota(jnp.int32, (128, 256), 0)

    def build_map(n, i):
        for k in range(2):
            gmap[n, :, k * 256 : (k + 1) * 256] = (slots[k] == rows_iota + i * 128).astype(F32).astype(BF)

    r_out = lax.broadcasted_iota(jnp.int32, (128, 128), 0)
    r_in = lax.broadcasted_iota(jnp.int32, (128, 128), 1)
    perm = (r_in == (r_out & 15) // 2 * 16 + (r_out >> 4) * 2 + (r_out & 1)).astype(F32).astype(BF)

    for g in range(GROUPS):
        build_map(g, c * GROUPS + g)

    pl.semaphore_wait(barrier, len(peers))
    tok_local.wait()
    tok_remote = remote(tokt.at[mine], tokt.at[mine], tsem.at[1], tsem.at[2], other)
    tok_remote.start()
    w_remote = remote(w_ref, ww.at[c], wsem.at[1], wsem.at[2], other)
    w_remote.start()
    for g in range(GROUPS):
        build_map(GROUPS + g, (1 - c) * GROUPS + g)
    remote(tokt.at[mine], tokt.at[theirs], tsem.at[1], tsem.at[2], other).wait_recv()

    def stage_a(u):
        g, f, n = UNITS[u]
        part = pl.ds(f, n)
        dispatch = gmap[g, :, :256] + gmap[g, :, 256:]
        rows = dot(dispatch, tokt[f : f + n, :], ((1,), (1,))).astype(BF)
        ysend[g, :, :, part] = rows.reshape(8, 16, n)
        for j, p in ypeers:
            remote(ysend.at[g, j, :, part], yrecv.at[g, y, :, part], ysem.at[0, u], ysem.at[1, u], p).start()
        yrecv[g, y, :, part] = ysend[g, y, :, part]

    def y_done(u):
        g, f, n = UNITS[u]
        part = pl.ds(f, n)
        return remote(
            ysend.at[g, pl.ds(0, 7), :, part], yrecv.at[g, pl.ds(0, 7), :, part], ysem.at[0, u], ysem.at[1, u], other
        )

    def stage_b(u):
        g, f, n = UNITS[u]
        part = pl.ds(f, n)
        y_done(u).wait_recv()
        rows = yrecv[g, :, :, part].reshape(128, n)
        xsend[g, :, :, :, part] = dot(perm, rows, ((1,), (0,))).astype(BF).reshape(4, 2, 16, n)
        for j, p in xpeers:
            remote(xsend.at[g, j, 0, :, part], xf.at[g, h, 0, x, :, part], xsem.at[0, u], xsem.at[1, u], p).start()
            remote(xsend.at[g, j, 1, :, part], fs.at[g, x, :, part], xsem.at[2, u], xsem.at[3, u], p).start()
        xf[g, h, 0, x, :, part] = xsend[g, x, 0, :, part]
        fs[g, x, :, part] = xsend[g, x, 1, :, part]

    def x_done(u, k):
        g, f, n = UNITS[u]
        part = pl.ds(f, n)
        three = fs.at[g, pl.ds(0, 3), :, part]
        return remote(three, three, xsem.at[2 * k, u], xsem.at[2 * k + 1, u], other)

    def z_copies(u):
        g, f, n = UNITS[u]
        part = pl.ds(f, n)

        def near(o):
            return xf.at[g, o, 0, :, :, part]

        def half(o, k):
            return xf.at[g, o, 0, pl.ds(2 * k, 2), :, part]

        def far(o):
            return xf.at[g, o, 1, :, :, part]

        mod = lambda v: lax.rem(v, 4)
        out = [
            (near(h), near(h), zp2), (near(h), near(h), zm2),
            (fs.at[g, :, :, part], far(h), zp1), (fs.at[g, :, :, part], far(h), zm1),
            (half(mod(h + 3), 0), half(mod(h + 3), 0), zp2), (half(mod(h + 1), 1), half(mod(h + 1), 1), zm2),
            (far(mod(h + zl + 3)), far(mod(h + zl + 3)), zp2), (far(mod(h + zl)), far(mod(h + zl)), zm2),
        ]
        inn = [
            near(mod(h + 3)), near(mod(h + 1)), far(mod(h + zl + 3)), far(mod(h + zl)),
            half(mod(h + 2), 0), half(mod(h + 2), 1), far(mod(h + zl + 2)), far(mod(h + zl + 1)),
        ]
        return (
            lambda k: remote(out[k][0], out[k][1], zsend.at[k, u], zrecv.at[k, u], out[k][2]),
            lambda k: remote(inn[k], inn[k], zsend.at[k, u], zrecv.at[k, u], other),
        )

    def stage_c(u):
        out, _ = z_copies(u)
        x_done(u, 1).wait_recv()
        out(2).start()
        out(3).start()
        x_done(u, 0).wait_recv()
        out(0).start()
        out(1).start()

    def stage_d(u):
        out, inn = z_copies(u)
        for k, m in ((2, 6), (3, 7), (0, 4), (1, 5)):
            inn(k).wait_recv()
            out(m).start()

    def stage_e(u):
        g, f, n = UNITS[u]
        _, inn = z_copies(u)
        for k in (6, 7, 4, 5):
            inn(k).wait_recv()
        if f == 0:
            acc[...] = jnp.zeros_like(acc)

        def origin(o, carry):
            rows = xf[g, o, :, :, :, pl.ds(f, n)].reshape(128, n)
            cols = pl.ds(pl.multiple_of(o * LANES + f, 128), n)
            for j in range(2):
                acc[j] += dot(rows, ww[j, :, cols], ((1,), (1,)))
            return carry

        lax.fori_loop(0, 4, origin, 0)

    def stage_r1(g):
        for j in range(2):
            gate, up = acc[j, :, :WIDTH], acc[j, :, WIDTH:]
            value = (gate / (1.0 + jnp.exp(-gate)) * up).astype(BF)
            hb[g, :, :, :, j * WIDTH : (j + 1) * WIDTH] = value.reshape(2, 4, 16, WIDTH)
        for j, fl, p in qpeers:
            remote(hb.at[g, fl, j], rx.at[g, x, fl], r1sem.at[0, g], r1sem.at[1, g], p).start()
        rx[g, x, 0] = hb[g, 0, x]

    def r1_done(g):
        seven = ry.at[g, pl.ds(0, 7)]
        return remote(seven, seven, r1sem.at[0, g], r1sem.at[1, g], other)

    def stage_r2(g):
        r1_done(g).wait_recv()
        rows = rx[g].reshape(128, RET)
        rys[g] = dot(perm, rows, ((1,), (0,))).astype(BF).reshape(8, 16, RET)
        for j, p in ypeers:
            remote(rys.at[g, j], ry.at[g, y], r2sem.at[0, g], r2sem.at[1, g], p).start()
        ry[g, y] = rys[g, y]

    def r2_done(g):
        seven = ry.at[g, pl.ds(0, 7)]
        return remote(seven, seven, r2sem.at[0, g], r2sem.at[1, g], other)

    def r3_copy(g):
        cols = pl.ds(pl.multiple_of((1 - c) * 256, 128), OUTW)
        return remote(ry.at[g, :, :, cols], rd.at[g], r3sem.at[0, g], r3sem.at[1, g], other)

    def stage_r3(g):
        r2_done(g).wait_recv()
        r3_copy(g).start()
        own = ry[g, :, :, pl.ds(pl.multiple_of(c * 256, 128), OUTW)].reshape(128, OUTW)
        part = dot(own, gmap[g], ((0,), (0,)))
        oacc[...] = part if g == 0 else oacc[...] + part

    def stage_r4(g):
        r3_copy(g).wait_recv()
        oacc[...] += dot(rd[g].reshape(128, OUTW), gmap[GROUPS + g], ((0,), (0,)))

    hb[...] = jnp.zeros_like(hb)
    stage_a(0)
    stage_a(1)
    stage_b(0)
    stage_a(2)
    stage_c(0)
    stage_b(1)
    stage_a(3)
    stage_c(1)
    stage_b(2)
    stage_a(4)
    stage_d(0)
    stage_c(2)
    stage_b(3)
    stage_a(5)
    w_local.wait()
    w_remote.wait()
    stage_d(1)
    stage_c(3)
    stage_e(0)
    stage_b(4)
    stage_d(2)
    stage_c(4)
    stage_e(1)
    stage_r1(0)
    stage_b(5)
    stage_d(3)
    stage_c(5)
    stage_r2(0)
    stage_e(2)
    stage_d(4)
    stage_r3(0)
    stage_e(3)
    stage_r1(1)
    stage_d(5)
    stage_r4(0)
    stage_e(4)
    stage_r2(1)
    stage_e(5)
    stage_r1(2)
    stage_r3(1)
    stage_r4(1)
    stage_r2(2)
    stage_r3(2)
    stage_r4(2)
    start = pl.multiple_of(c * 48, 16)
    for k in range(2):
        out_ref[k] = oacc[pl.ds(start, WIDTH), k * 256 : (k + 1) * 256].astype(BF)

    tok_remote.wait_send()
    for u in range(len(UNITS)):
        y_done(u).wait_send()
        x_done(u, 0).wait_send()
        x_done(u, 1).wait_send()
        for k in range(8):
            z_copies(u)[0](k).wait_send()
    for g in range(GROUPS):
        r1_done(g).wait_send()
        r2_done(g).wait_send()
        r3_copy(g).wait_send()


def shards(tokens, expert_ids, weights):
    tok = tokens.T
    ids = expert_ids.T
    w = weights.transpose(0, 2, 3, 1).reshape(2 * WIDTH, weights.shape[1])
    units = len(UNITS)
    vmem = pltpu.VMEM
    dma = pltpu.SemaphoreType.DMA
    out = pl.pallas_call(
        kernel,
        out_shape=jax.ShapeDtypeStruct((2, WIDTH, 256), BF),
        in_specs=[
            pl.BlockSpec(memory_space=pltpu.VMEM),
            pl.BlockSpec(memory_space=pl.ANY),
            pl.BlockSpec(memory_space=pl.ANY),
        ],
        out_specs=pl.BlockSpec(memory_space=pltpu.VMEM),
        scratch_shapes=[
            vmem((LANES, 256), BF),
            vmem((2, 2 * WIDTH, 3584), BF),
            vmem((GROUPS, 8, 16, LANES), BF),
            vmem((GROUPS, 8, 16, LANES), BF),
            vmem((GROUPS, 4, 2, 16, LANES), BF),
            vmem((GROUPS, 4, 16, LANES), BF),
            vmem((GROUPS, 4, 2, 4, 16, LANES), BF),
            vmem((2, 128, 2 * WIDTH), F32),
            vmem((GROUPS, 2, 4, 16, RET), BF),
            vmem((GROUPS, 4, 2, 16, RET), BF),
            vmem((GROUPS, 8, 16, RET), BF),
            vmem((GROUPS, 8, 16, RET), BF),
            vmem((GROUPS, 8, 16, OUTW), BF),
            vmem((2 * GROUPS, 128, 512), BF),
            vmem((OUTW, 512), F32),
            dma((3,)),
            dma((3,)),
            dma((1,)),
            dma((2, units)),
            dma((4, units)),
            dma((8, units)),
            dma((8, units)),
            dma((2, GROUPS)),
            dma((2, GROUPS)),
            dma((2, GROUPS)),
        ],
        compiler_params=pltpu.CompilerParams(
            collective_id=1, has_side_effects=True, vmem_limit_bytes=56 << 20
        ),
        cost_estimate=pl.CostEstimate(flops=3355443200, bytes_accessed=5000000, transcendentals=233472),
        name="routed_projections",
    )(ids, tok, w)
    return out.transpose(2, 0, 1)


def solution(mesh):
    return jax.shard_map(
        shards,
        mesh=mesh,
        in_specs=(P("expert", "tensor"), P("expert", None), P("expert", None, None, "tensor")),
        out_specs=P("expert", None, "tensor"),
        check_vma=False,
    )
```

```python
import functools

import jax
import jax.numpy as jnp
from jax import lax
from jax.experimental import pallas as pl
from jax.experimental.pallas import tpu as pltpu
from jax.sharding import PartitionSpec as P

MESH = pl.DeviceIdType.MESH
BF = jnp.bfloat16
F32 = jnp.float32

GROUPS = 3
HALF = 448
AW = 384
BW = 512
BF_ROWS = 64
WIDTH = 304
RET = 384
UNITS = [(0, 0), (0, 1), (1, 0), (1, 1), (2, 0), (2, 1)]


def dot(a, b, dims):
    return lax.dot_general(a, b, (dims, ((), ())), preferred_element_type=F32)


def kernel(
    ids_ref, tok_ref, w_ref, out_ref,
    tokm, toko, tb, ido, ww, ysend, yrecv, xsend, fs, xf, ysb, yrb, xsb, xb,
    acc, hb, rx, rys, rd, gmap, bmap, oacc,
    tsem, wsem, bsem, ysem, xsem, zsend, zrecv, ybsem, xbsem, r1sem, r2sem,
):
    e = lax.axis_index("expert")
    t = lax.axis_index("tensor")
    y = lax.rem(e, 8)
    q = e // 8
    x = q // 2
    zl = lax.rem(q, 2)
    h = t // 2
    c = lax.rem(t, 2)

    def dev(x_, zl_, y_, h_):
        return ((x_ * 2 + zl_) * 8 + y_, h_ * 2 + c)

    def mod4(v):
        return lax.rem(v, 4)

    def across(d):
        return (d[0], d[1] + 1 - 2 * c)

    other = across((e, t))
    zp1 = dev(x, 1 - zl, y, mod4(h + zl))
    zm1 = dev(x, 1 - zl, y, mod4(h + zl + 3))
    zp2 = dev(x, zl, y, mod4(h + 1))
    zm2 = dev(x, zl, y, mod4(h + 3))
    zp3 = dev(x, 1 - zl, y, mod4(h + zl + 1))
    zm3 = dev(x, 1 - zl, y, mod4(h + zl + 2))
    zp4 = dev(x, zl, y, mod4(h + 2))
    line = [zp1, zm1, zp2, zm2, zp3, zm3, zp4]
    ypeers = [(lax.rem(y + d, 8), dev(x, zl, lax.rem(y + d, 8), h)) for d in (4, 3, 5, 2, 6, 1, 7)]
    xpeers = [(mod4(x + d), dev(mod4(x + d), zl, y, h)) for d in (2, 1, 3)]
    qpeers = [
        (mod4(x + d), f, dev(mod4(x + d), (1 - zl) if f else zl, y, h))
        for d, f in ((2, 1), (1, 1), (3, 1), (2, 0), (1, 0), (3, 0), (0, 1))
    ]
    twin = dev(x, 1 - zl, y, h)

    barrier = pltpu.get_barrier_semaphore()
    peers = [p for _, p in ypeers] + [across(p) for _, p in ypeers] + [p for _, _, p in qpeers] + line + [other]
    for p in peers:
        pl.semaphore_signal(barrier, inc=1, device_id=p, device_id_type=MESH)

    def remote(src, dst, ss, rs, p):
        return pltpu.make_async_remote_copy(
            src_ref=src, dst_ref=dst, send_sem=ss, recv_sem=rs, device_id=p, device_id_type=MESH
        )

    tok_local = pltpu.make_async_copy(tok_ref, tokm, tsem.at[0])
    tok_local.start()
    w_local = pltpu.make_async_copy(w_ref, ww.at[0], wsem.at[0])
    w_local.start()

    experts = lax.broadcasted_iota(jnp.int32, (64, 256), 0)
    upper = (
        lax.broadcasted_iota(jnp.int32, (256, 256), 0) < lax.broadcasted_iota(jnp.int32, (256, 256), 1)
    ).astype(F32).astype(BF)

    def slots_of(ids, source_zl):
        counted = jnp.zeros((64, 1), F32)
        slots = []
        for k in range(2):
            expert = ids[k : k + 1, :]
            hot = (experts == expert).astype(F32)
            before = dot(hot.astype(BF), upper, ((1,), (0,))) + counted
            counted = counted + jnp.sum(hot, axis=1, keepdims=True)
            rank = jnp.sum(before * hot, axis=0, keepdims=True).astype(jnp.int32)
            ey, eq = expert & 7, expert >> 3
            flip = (eq + source_zl) & 1
            row = ey * 16 + (eq >> 1) * 4 + flip * 2 + ((rank >> 1) & 1)
            slots.append(((rank & 1) * GROUPS + (rank >> 2)) * 128 + row)
        return slots

    rows_iota = lax.broadcasted_iota(jnp.int32, (128, 256), 0)
    slots = slots_of(ids_ref, zl)

    def build_map(g, k):
        wanted = rows_iota + ((c if k == 0 else 1 - c) * GROUPS + g) * 128
        for choice in range(2):
            gmap[g, k, :, choice * 256 : (choice + 1) * 256] = (slots[choice] == wanted).astype(F32).astype(BF)

    r_out = lax.broadcasted_iota(jnp.int32, (128, 128), 0)
    r_in = lax.broadcasted_iota(jnp.int32, (128, 128), 1)
    perm = (r_in == (r_out & 15) // 2 * 16 + (r_out >> 4) * 2 + (r_out & 1)).astype(F32).astype(BF)

    build_map(0, 0)

    b_rows = pl.ds(pl.multiple_of((1 - c) * AW, 16), BF_ROWS)
    b_dst = pl.ds(pl.multiple_of(c * BF_ROWS, 16), BF_ROWS)
    a_rows = pl.ds(pl.multiple_of(c * BF_ROWS, 16), AW)

    tok_local.wait()
    pl.semaphore_wait(barrier, len(peers))
    tok_remote = remote(tokm.at[a_rows], toko, tsem.at[1], tsem.at[2], other)
    tok_remote.start()
    ids_remote = remote(ids_ref, ido, bsem.at[0], bsem.at[1], twin)
    ids_remote.start()

    def stage_s(_):
        for p in line:
            remote(tokm.at[b_rows], tb.at[zl, h, b_dst], bsem.at[2], bsem.at[3], p).start()
        tb[zl, h, b_dst] = tokm[b_rows]

    def s_done():
        n = BF_ROWS * 7
        return remote(tokm.at[pl.ds(0, n)], tokm.at[pl.ds(0, n)], bsem.at[2], bsem.at[3], other)

    def pass_copy():
        return remote(tb.at[:, :, b_dst], tb.at[:, :, b_dst], bsem.at[4], bsem.at[5], other)

    def stage_t(_):
        s_done().wait_recv()
        pass_copy().start()

    def stage_m(k):
        for g in range(1 - k, GROUPS):
            build_map(g, k)

    def stage_n(_):
        ids_remote.wait_recv()
        theirs = slots_of(ido, 1 - zl)
        flips = (rows_iota >> 1) & 1
        for g in range(GROUPS):
            wanted = rows_iota + (c * GROUPS + g) * 128
            here = (gmap[g, 0, :, :256] + gmap[g, 0, :, 256:]).astype(F32)
            there = jnp.where((theirs[0] == wanted) | (theirs[1] == wanted), 1.0, 0.0)
            bmap[g, :, :256] = jnp.where(flips == 0, here, 0.0).astype(BF)
            bmap[g, :, 256:] = jnp.where(flips == 1, there, 0.0).astype(BF)

    def stage_a(u):
        g, p = UNITS[u]
        dispatch = gmap[g, 0, :, :256] + gmap[g, 0, :, 256:]
        if u == 1:
            remote(toko, toko, tsem.at[1], tsem.at[2], other).wait_recv()
        features = tokm[a_rows] if p == 0 else toko[...]
        ysend[p, g] = dot(dispatch, features, ((1,), (1,))).astype(BF).reshape(8, 16, AW)
        for j, d in ypeers:
            remote(ysend.at[p, g, j], yrecv.at[p, g, y], ysem.at[0, u], ysem.at[1, u], d).start()
        yrecv[p, g, y] = ysend[p, g, y]

    def y_done(u):
        g, p = UNITS[u]
        seven = yrecv.at[p, g, pl.ds(0, 7)]
        return remote(seven, seven, ysem.at[0, u], ysem.at[1, u], other)

    def stage_b(u):
        g, p = UNITS[u]
        y_done(u).wait_recv()
        rows = yrecv[p, g].reshape(128, AW)
        xsend[p, g] = dot(perm, rows, ((1,), (0,))).astype(BF).reshape(4, 2, 16, AW)
        for j, d in xpeers:
            remote(xsend.at[p, g, j, 1], fs.at[p, g, x], xsem.at[2, u], xsem.at[3, u], d).start()
        for j, d in xpeers:
            remote(xsend.at[p, g, j, 0], xf.at[p, g, h, 0, x], xsem.at[0, u], xsem.at[1, u], d).start()
        xf[p, g, h, 0, x] = xsend[p, g, x, 0]
        fs[p, g, x] = xsend[p, g, x, 1]

    def x_done(u, k):
        g, p = UNITS[u]
        three = fs.at[p, g, pl.ds(0, 3)]
        return remote(three, three, xsem.at[2 * k, u], xsem.at[2 * k + 1, u], other)

    def z_copies(u):
        g, p = UNITS[u]

        def near(o):
            return xf.at[p, g, o, 0]

        def half(o, k):
            return xf.at[p, g, o, 0, pl.ds(2 * k, 2)]

        def far(o):
            return xf.at[p, g, o, 1]

        out = [
            (near(h), near(h), zp2), (near(h), near(h), zm2),
            (fs.at[p, g], far(h), zp1), (fs.at[p, g], far(h), zm1),
            (half(mod4(h + 3), 0), half(mod4(h + 3), 0), zp2), (half(mod4(h + 1), 1), half(mod4(h + 1), 1), zm2),
            (far(mod4(h + zl + 3)), far(mod4(h + zl + 3)), zp2), (far(mod4(h + zl)), far(mod4(h + zl)), zm2),
        ]
        inn = [
            near(mod4(h + 3)), near(mod4(h + 1)), far(mod4(h + zl + 3)), far(mod4(h + zl)),
            half(mod4(h + 2), 0), half(mod4(h + 2), 1), far(mod4(h + zl + 2)), far(mod4(h + zl + 1)),
        ]
        return (
            lambda k: remote(out[k][0], out[k][1], zsend.at[k, u], zrecv.at[k, u], out[k][2]),
            lambda k: remote(inn[k], inn[k], zsend.at[k, u], zrecv.at[k, u], other),
        )

    def stage_c(u):
        out, _ = z_copies(u)
        x_done(u, 1).wait_recv()
        out(2).start()
        out(3).start()
        x_done(u, 0).wait_recv()
        out(0).start()
        out(1).start()

    def stage_d(u):
        out, inn = z_copies(u)
        for k, m in ((2, 6), (3, 7), (0, 4), (1, 5)):
            inn(k).wait_recv()
            out(m).start()

    def stage_e(u):
        stage_w(u)
        for k in range(2):
            stage_f(u, k)

    def stage_w(u):
        _, inn = z_copies(u)
        for k in (6, 7, 4, 5):
            inn(k).wait_recv()

    def stage_f(u, k):
        g, p = UNITS[u]
        first = (c if p == 0 else 1 - c) * BW
        total = jnp.zeros((2 * WIDTH, 128), F32) if p == 0 else acc[k]
        for o in range(4):
            cols = pl.ds(pl.multiple_of(o * 2 * HALF + first, 128), AW)
            total = total + dot(ww[k, :, cols], xf[p, g, o].reshape(128, AW), ((1,), (1,)))
        acc[k] = total

    def stage_ab(g):
        if g == 0:
            pass_copy().wait_recv()
        rows = jnp.zeros((128, BW), F32)
        for s, plane in ((0, zl), (1, 1 - zl)):
            features = tb[plane].reshape(BW, 256)
            rows = rows + dot(bmap[g, :, s * 256 : (s + 1) * 256], features, ((1,), (1,)))
        ysb[g] = rows.astype(BF).reshape(8, 16, BW)
        for j, d in ypeers:
            remote(ysb.at[g, j], yrb.at[g, y], ybsem.at[0, g], ybsem.at[1, g], d).start()
        yrb[g, y] = ysb[g, y]

    def yb_done(g):
        seven = yrb.at[g, pl.ds(0, 7)]
        return remote(seven, seven, ybsem.at[0, g], ybsem.at[1, g], other)

    def stage_bb(g):
        yb_done(g).wait_recv()
        rows = yrb[g].reshape(128, BW)
        xsb[g] = dot(perm, rows, ((1,), (0,))).astype(BF).reshape(4, 2, 16, BW)
        for j, d in xpeers:
            remote(xsb.at[g, j], xb.at[g, x], xbsem.at[0, g], xbsem.at[1, g], d).start()
        xb[g, x] = xsb[g, x]

    def xb_done(g):
        three = xb.at[g, pl.ds(0, 3)]
        return remote(three, three, xbsem.at[0, g], xbsem.at[1, g], other)

    def stage_eb(g):
        xb_done(g).wait_recv()
        for k in range(2):
            total = acc[k]
            for o in range(4):
                lanes = slice(o * 128, (o + 1) * 128)
                rows = jnp.concatenate([xb[g, :, f, :, lanes].reshape(64, 128) for f in range(2)])
                cols = slice(o * 2 * HALF + AW, o * 2 * HALF + BW)
                total = total + dot(ww[k, :, cols], rows, ((1,), (1,)))
            acc[k] = total

    def stage_r1(g):
        for k in range(2):
            stage_h(g, k)

    def stage_h(g, k):
        gate, up = acc[k, :WIDTH, :], acc[k, WIDTH:, :]
        value = gate / (1.0 + jnp.exp(-gate)) * up
        value = jnp.concatenate([value, jnp.zeros((RET - WIDTH, 128), F32)])
        hb[k, g] = value.T.astype(BF).reshape(2, 4, 16, RET)
        for j, fl, p in qpeers:
            remote(hb.at[k, g, fl, j], rx.at[k, g, x, fl], r1sem.at[0, k, g], r1sem.at[1, k, g], p).start()
        rx[k, g, x, 0] = hb[k, g, 0, x]

    def r1_done(g, k):
        seven = rd.at[g, pl.ds(0, 7)]
        return remote(seven, seven, r1sem.at[0, k, g], r1sem.at[1, k, g], other)

    def stage_r2(g):
        for k in range(2):
            stage_k(g, k)

    def stage_k(g, k):
        r1_done(g, k).wait_recv()
        rows = rx[k, g].reshape(128, RET)
        rys[k, g] = dot(perm, rows, ((1,), (0,))).astype(BF).reshape(8, 16, RET)
        for j, p in ypeers:
            to = p if k == 0 else across(p)
            remote(rys.at[k, g, j], rd.at[g, k * 8 + y], r2sem.at[0, g], r2sem.at[1, g], to).start()
        if k == 0:
            rd[g, y] = rys[0, g, y]
        else:
            remote(rys.at[1, g, y], rd.at[g, 8 + y], r2sem.at[0, g], r2sem.at[1, g], other).start()

    def r2_done(g):
        fifteen = rd.at[g, pl.ds(0, 15)]
        return remote(fifteen, fifteen, r2sem.at[0, g], r2sem.at[1, g], other)

    def stage_r4(g):
        r2_done(g).wait_recv()
        part = dot(rd[g].reshape(256, RET), gmap[g].reshape(256, 512), ((0,), (0,)))
        oacc[...] = part if g == 0 else oacc[...] + part

    stage_a(0)
    stage_s(0)
    stage_m(0)
    stage_a(1)
    w_remote = remote(w_ref, ww.at[1], wsem.at[1], wsem.at[2], other)
    w_remote.start()
    stage_a(2)
    stage_b(0)
    stage_c(0)
    stage_a(3)
    stage_b(1)
    stage_c(1)
    stage_n(0)
    stage_a(4)
    stage_b(2)
    stage_d(0)
    stage_c(2)
    stage_a(5)
    stage_b(3)
    stage_t(0)
    stage_d(1)
    stage_c(3)
    stage_ab(0)
    stage_m(1)
    stage_b(4)
    stage_ab(1)
    w_local.wait()
    w_remote.wait()
    stage_e(0)
    stage_d(2)
    stage_c(4)
    stage_b(5)
    stage_ab(2)
    stage_bb(0)
    stage_e(1)
    stage_eb(0)
    stage_r1(0)
    stage_d(3)
    stage_c(5)
    stage_bb(1)
    stage_e(2)
    stage_d(4)
    stage_r2(0)
    stage_e(3)
    stage_eb(1)
    stage_r1(1)
    stage_bb(2)
    stage_d(5)
    stage_e(4)
    stage_eb(2)
    stage_r2(1)
    stage_r4(0)
    stage_w(5)
    stage_f(5, 0)
    stage_h(2, 0)
    stage_f(5, 1)
    stage_h(2, 1)
    stage_r4(1)
    stage_k(2, 0)
    stage_k(2, 1)
    stage_r4(2)
    for k in range(2):
        out_ref[k] = oacc[:WIDTH, k * 256 : (k + 1) * 256].astype(BF)

    tok_remote.wait_send()
    ids_remote.wait_send()
    s_done().wait_send()
    pass_copy().wait_send()
    for u in range(len(UNITS)):
        y_done(u).wait_send()
        x_done(u, 0).wait_send()
        x_done(u, 1).wait_send()
        for k in range(8):
            z_copies(u)[0](k).wait_send()
    for g in range(GROUPS):
        yb_done(g).wait_send()
        xb_done(g).wait_send()
        r1_done(g, 0).wait_send()
        r1_done(g, 1).wait_send()
        r2_done(g).wait_send()


def shards(tokens, expert_ids, weights):
    tok = tokens.T
    ids = expert_ids.T
    w = weights.transpose(0, 2, 3, 1).reshape(2 * WIDTH, weights.shape[1])
    units = len(UNITS)
    vmem = pltpu.VMEM
    dma = pltpu.SemaphoreType.DMA
    out = pl.pallas_call(
        kernel,
        out_shape=jax.ShapeDtypeStruct((2, WIDTH, 256), BF),
        in_specs=[
            pl.BlockSpec(memory_space=pltpu.VMEM),
            pl.BlockSpec(memory_space=pl.ANY),
            pl.BlockSpec(memory_space=pl.ANY),
        ],
        out_specs=pl.BlockSpec(memory_space=pltpu.VMEM),
        scratch_shapes=[
            vmem((HALF, 256), BF),
            vmem((AW, 256), BF),
            vmem((2, 4, 2 * BF_ROWS, 256), BF),
            vmem((2, 256), jnp.int32),
            vmem((2, 2 * WIDTH, 3584), BF),
            vmem((2, GROUPS, 8, 16, AW), BF),
            vmem((2, GROUPS, 8, 16, AW), BF),
            vmem((2, GROUPS, 4, 2, 16, AW), BF),
            vmem((2, GROUPS, 4, 16, AW), BF),
            vmem((2, GROUPS, 4, 2, 4, 16, AW), BF),
            vmem((GROUPS, 8, 16, BW), BF),
            vmem((GROUPS, 8, 16, BW), BF),
            vmem((GROUPS, 4, 2, 16, BW), BF),
            vmem((GROUPS, 4, 2, 16, BW), BF),
            vmem((2, 2 * WIDTH, 128), F32),
            vmem((2, GROUPS, 2, 4, 16, RET), BF),
            vmem((2, GROUPS, 4, 2, 16, RET), BF),
            vmem((2, GROUPS, 8, 16, RET), BF),
            vmem((GROUPS, 16, 16, RET), BF),
            vmem((GROUPS, 2, 128, 512), BF),
            vmem((GROUPS, 128, 512), BF),
            vmem((RET, 512), F32),
            dma((3,)),
            dma((3,)),
            dma((6,)),
            dma((2, units)),
            dma((4, units)),
            dma((8, units)),
            dma((8, units)),
            dma((2, GROUPS)),
            dma((2, GROUPS)),
            dma((2, 2, GROUPS)),
            dma((2, GROUPS)),
        ],
        compiler_params=pltpu.CompilerParams(
            collective_id=1, has_side_effects=True, vmem_limit_bytes=56 << 20
        ),
        cost_estimate=pl.CostEstimate(flops=3355443200, bytes_accessed=5000000, transcendentals=233472),
        name="routed_projections",
    )(ids, tok, w)
    return out.transpose(2, 0, 1)


def solution(mesh):
    return jax.shard_map(
        shards,
        mesh=mesh,
        in_specs=(P("expert", "tensor"), P("expert", None), P("expert", None, None, "tensor")),
        out_specs=P("expert", None, "tensor"),
        check_vma=False,
    )
```

```python
import functools

import jax
import jax.numpy as jnp
from jax import lax
from jax.experimental import pallas as pl
from jax.experimental.pallas import tpu as pltpu
from jax.sharding import PartitionSpec as P

MESH = pl.DeviceIdType.MESH
BF = jnp.bfloat16
F32 = jnp.float32

GROUPS = 3
HALF = 448
AW = 384
BW = 512
BF_ROWS = 64
WIDTH = 304
RET = 384
UNITS = [(0, 0), (0, 1), (1, 0), (1, 1), (2, 0), (2, 1)]


def dot(a, b, dims):
    return lax.dot_general(a, b, (dims, ((), ())), preferred_element_type=F32)


def kernel(
    ids_ref, tok_ref, w_ref, out_ref,
    tokm, toko, tb, ido, ww, ysend, yrecv, xsend, fs, xf, ysb, yrb, xsb, xb,
    acc, hb, rx, rys, rd, gmap, bmap, oacc,
    tsem, wsem, bsem, ysem, xsem, zsend, zrecv, ybsem, xbsem, r1sem, r2sem,
):
    e = lax.axis_index("expert")
    t = lax.axis_index("tensor")
    y = lax.rem(e, 8)
    q = e // 8
    x = q // 2
    zl = lax.rem(q, 2)
    h = t // 2
    c = lax.rem(t, 2)

    def dev(x_, zl_, y_, h_):
        return ((x_ * 2 + zl_) * 8 + y_, h_ * 2 + c)

    def mod4(v):
        return lax.rem(v, 4)

    def across(d):
        return (d[0], d[1] + 1 - 2 * c)

    other = across((e, t))
    zp1 = dev(x, 1 - zl, y, mod4(h + zl))
    zm1 = dev(x, 1 - zl, y, mod4(h + zl + 3))
    zp2 = dev(x, zl, y, mod4(h + 1))
    zm2 = dev(x, zl, y, mod4(h + 3))
    zp3 = dev(x, 1 - zl, y, mod4(h + zl + 1))
    zm3 = dev(x, 1 - zl, y, mod4(h + zl + 2))
    zp4 = dev(x, zl, y, mod4(h + 2))
    line = [zp1, zm1, zp2, zm2, zp3, zm3, zp4]
    ypeers = [(lax.rem(y + d, 8), dev(x, zl, lax.rem(y + d, 8), h)) for d in (4, 3, 5, 2, 6, 1, 7)]
    xpeers = [(mod4(x + d), dev(mod4(x + d), zl, y, h)) for d in (2, 1, 3)]
    qpeers = [
        (mod4(x + d), f, dev(mod4(x + d), (1 - zl) if f else zl, y, h))
        for d, f in ((2, 1), (1, 1), (3, 1), (2, 0), (1, 0), (3, 0), (0, 1))
    ]
    twin = dev(x, 1 - zl, y, h)

    barrier = pltpu.get_barrier_semaphore()
    peers = [p for _, p in ypeers] + [across(p) for _, p in ypeers] + [p for _, _, p in qpeers] + line + [other]
    for p in peers:
        pl.semaphore_signal(barrier, inc=1, device_id=p, device_id_type=MESH)

    def remote(src, dst, ss, rs, p):
        return pltpu.make_async_remote_copy(
            src_ref=src, dst_ref=dst, send_sem=ss, recv_sem=rs, device_id=p, device_id_type=MESH
        )

    tok_local = pltpu.make_async_copy(tok_ref, tokm, tsem.at[0])
    tok_local.start()
    w_local = pltpu.make_async_copy(w_ref, ww.at[0], wsem.at[0])
    w_local.start()

    experts = lax.broadcasted_iota(jnp.int32, (64, 256), 0)
    upper = (
        lax.broadcasted_iota(jnp.int32, (256, 256), 0) < lax.broadcasted_iota(jnp.int32, (256, 256), 1)
    ).astype(F32).astype(BF)

    def slots_of(ids, source_zl):
        counted = jnp.zeros((64, 1), F32)
        slots = []
        for k in range(2):
            expert = ids[k : k + 1, :]
            hot = (experts == expert).astype(F32)
            before = dot(hot.astype(BF), upper, ((1,), (0,))) + counted
            counted = counted + jnp.sum(hot, axis=1, keepdims=True)
            rank = jnp.sum(before * hot, axis=0, keepdims=True).astype(jnp.int32)
            ey, eq = expert & 7, expert >> 3
            flip = (eq + source_zl) & 1
            row = ey * 16 + (eq >> 1) * 4 + flip * 2 + ((rank >> 1) & 1)
            slots.append(((rank & 1) * GROUPS + (rank >> 2)) * 128 + row)
        return slots

    rows_iota = lax.broadcasted_iota(jnp.int32, (128, 256), 0)
    slots = slots_of(ids_ref, zl)

    def build_map(g, k):
        wanted = rows_iota + ((c if k == 0 else 1 - c) * GROUPS + g) * 128
        for choice in range(2):
            gmap[g, k, :, choice * 256 : (choice + 1) * 256] = (slots[choice] == wanted).astype(F32).astype(BF)

    r_out = lax.broadcasted_iota(jnp.int32, (128, 128), 0)
    r_in = lax.broadcasted_iota(jnp.int32, (128, 128), 1)
    perm = (r_in == (r_out & 15) // 2 * 16 + (r_out >> 4) * 2 + (r_out & 1)).astype(F32).astype(BF)

    build_map(0, 0)

    b_rows = pl.ds(pl.multiple_of((1 - c) * AW, 16), BF_ROWS)
    b_dst = pl.ds(pl.multiple_of(c * BF_ROWS, 16), BF_ROWS)
    a_rows = pl.ds(pl.multiple_of(c * BF_ROWS, 16), AW)

    tok_local.wait()
    pl.semaphore_wait(barrier, len(peers))
    tok_remote = remote(tokm.at[a_rows], toko, tsem.at[1], tsem.at[2], other)
    tok_remote.start()
    ids_remote = remote(ids_ref, ido, bsem.at[0], bsem.at[1], twin)
    ids_remote.start()

    def stage_s(_):
        for p in line:
            remote(tokm.at[b_rows], tb.at[zl, h, b_dst], bsem.at[2], bsem.at[3], p).start()
        tb[zl, h, b_dst] = tokm[b_rows]

    def s_done():
        n = BF_ROWS * 7
        return remote(tokm.at[pl.ds(0, n)], tokm.at[pl.ds(0, n)], bsem.at[2], bsem.at[3], other)

    def pass_copy():
        return remote(tb.at[:, :, b_dst], tb.at[:, :, b_dst], bsem.at[4], bsem.at[5], other)

    def stage_t(_):
        s_done().wait_recv()
        pass_copy().start()

    def stage_m(k):
        for g in range(1 - k, GROUPS):
            build_map(g, k)

    def stage_n(_):
        ids_remote.wait_recv()
        theirs = slots_of(ido, 1 - zl)
        flips = (rows_iota >> 1) & 1
        for g in range(GROUPS):
            wanted = rows_iota + (c * GROUPS + g) * 128
            here = (gmap[g, 0, :, :256] + gmap[g, 0, :, 256:]).astype(F32)
            there = jnp.where((theirs[0] == wanted) | (theirs[1] == wanted), 1.0, 0.0)
            bmap[g, :, :256] = jnp.where(flips == 0, here, 0.0).astype(BF)
            bmap[g, :, 256:] = jnp.where(flips == 1, there, 0.0).astype(BF)

    def stage_a(u):
        g, p = UNITS[u]
        dispatch = gmap[g, 0, :, :256] + gmap[g, 0, :, 256:]
        if u == 1:
            remote(toko, toko, tsem.at[1], tsem.at[2], other).wait_recv()
        features = tokm[a_rows] if p == 0 else toko[...]
        ysend[p, g] = dot(dispatch, features, ((1,), (1,))).astype(BF).reshape(8, 16, AW)
        for j, d in ypeers:
            remote(ysend.at[p, g, j], yrecv.at[p, g, y], ysem.at[0, u], ysem.at[1, u], d).start()
        yrecv[p, g, y] = ysend[p, g, y]

    def y_done(u):
        g, p = UNITS[u]
        seven = yrecv.at[p, g, pl.ds(0, 7)]
        return remote(seven, seven, ysem.at[0, u], ysem.at[1, u], other)

    def stage_b(u):
        g, p = UNITS[u]
        y_done(u).wait_recv()
        rows = yrecv[p, g].reshape(128, AW)
        xsend[p, g] = dot(perm, rows, ((1,), (0,))).astype(BF).reshape(4, 2, 16, AW)
        for j, d in xpeers:
            remote(xsend.at[p, g, j, 1], fs.at[p, g, x], xsem.at[2, u], xsem.at[3, u], d).start()
        for j, d in xpeers:
            remote(xsend.at[p, g, j, 0], xf.at[p, g, h, 0, x], xsem.at[0, u], xsem.at[1, u], d).start()
        xf[p, g, h, 0, x] = xsend[p, g, x, 0]
        fs[p, g, x] = xsend[p, g, x, 1]

    def x_done(u, k):
        g, p = UNITS[u]
        three = fs.at[p, g, pl.ds(0, 3)]
        return remote(three, three, xsem.at[2 * k, u], xsem.at[2 * k + 1, u], other)

    def z_copies(u):
        g, p = UNITS[u]

        def near(o):
            return xf.at[p, g, o, 0]

        def half(o, k):
            return xf.at[p, g, o, 0, pl.ds(2 * k, 2)]

        def far(o):
            return xf.at[p, g, o, 1]

        out = [
            (near(h), near(h), zp2), (near(h), near(h), zm2),
            (fs.at[p, g], far(h), zp1), (fs.at[p, g], far(h), zm1),
            (half(mod4(h + 3), 0), half(mod4(h + 3), 0), zp2), (half(mod4(h + 1), 1), half(mod4(h + 1), 1), zm2),
            (far(mod4(h + zl + 3)), far(mod4(h + zl + 3)), zp2), (far(mod4(h + zl)), far(mod4(h + zl)), zm2),
        ]
        inn = [
            near(mod4(h + 3)), near(mod4(h + 1)), far(mod4(h + zl + 3)), far(mod4(h + zl)),
            half(mod4(h + 2), 0), half(mod4(h + 2), 1), far(mod4(h + zl + 2)), far(mod4(h + zl + 1)),
        ]
        return (
            lambda k: remote(out[k][0], out[k][1], zsend.at[k, u], zrecv.at[k, u], out[k][2]),
            lambda k: remote(inn[k], inn[k], zsend.at[k, u], zrecv.at[k, u], other),
        )

    def stage_c(u):
        out, _ = z_copies(u)
        x_done(u, 1).wait_recv()
        out(2).start()
        out(3).start()
        x_done(u, 0).wait_recv()
        out(0).start()
        out(1).start()

    def stage_d(u):
        out, inn = z_copies(u)
        for k, m in ((2, 6), (3, 7), (0, 4), (1, 5)):
            inn(k).wait_recv()
            out(m).start()

    def stage_e(u):
        stage_w(u)
        for k in range(2):
            stage_f(u, k)

    def stage_w(u):
        _, inn = z_copies(u)
        for k in (6, 7, 4, 5):
            inn(k).wait_recv()

    def stage_f(u, k):
        g, p = UNITS[u]
        first = (c if p == 0 else 1 - c) * BW
        total = jnp.zeros((2 * WIDTH, 128), F32) if p == 0 else acc[k]
        for o in range(4):
            cols = pl.ds(pl.multiple_of(o * 2 * HALF + first, 128), AW)
            total = total + dot(ww[k, :, cols], xf[p, g, o].reshape(128, AW), ((1,), (1,)))
        acc[k] = total

    def stage_ab(g):
        if g == 0:
            pass_copy().wait_recv()
        rows = jnp.zeros((128, BW), F32)
        for s, plane in ((0, zl), (1, 1 - zl)):
            features = tb[plane].reshape(BW, 256)
            rows = rows + dot(bmap[g, :, s * 256 : (s + 1) * 256], features, ((1,), (1,)))
        ysb[g] = rows.astype(BF).reshape(8, 16, BW)
        for j, d in ypeers:
            remote(ysb.at[g, j], yrb.at[g, y], ybsem.at[0, g], ybsem.at[1, g], d).start()
        yrb[g, y] = ysb[g, y]

    def yb_done(g):
        seven = yrb.at[g, pl.ds(0, 7)]
        return remote(seven, seven, ybsem.at[0, g], ybsem.at[1, g], other)

    def stage_bb(g):
        yb_done(g).wait_recv()
        rows = yrb[g].reshape(128, BW)
        xsb[g] = dot(perm, rows, ((1,), (0,))).astype(BF).reshape(4, 2, 16, BW)
        for j, d in xpeers:
            remote(xsb.at[g, j], xb.at[g, x], xbsem.at[0, g], xbsem.at[1, g], d).start()
        xb[g, x] = xsb[g, x]

    def xb_done(g):
        three = xb.at[g, pl.ds(0, 3)]
        return remote(three, three, xbsem.at[0, g], xbsem.at[1, g], other)

    def stage_eb(g):
        xb_done(g).wait_recv()
        for k in range(2):
            total = acc[k]
            for o in range(4):
                lanes = slice(o * 128, (o + 1) * 128)
                rows = jnp.concatenate([xb[g, :, f, :, lanes].reshape(64, 128) for f in range(2)])
                cols = slice(o * 2 * HALF + AW, o * 2 * HALF + BW)
                total = total + dot(ww[k, :, cols], rows, ((1,), (1,)))
            acc[k] = total

    def stage_r1(g):
        for k in range(2):
            stage_h(g, k)

    def stage_h(g, k):
        gate, up = acc[k, :WIDTH, :], acc[k, WIDTH:, :]
        value = gate / (1.0 + jnp.exp(-gate)) * up
        value = jnp.concatenate([value, jnp.zeros((RET - WIDTH, 128), F32)])
        hb[k, g] = value.T.astype(BF).reshape(2, 4, 16, RET)
        for j, fl, p in qpeers:
            remote(hb.at[k, g, fl, j], rx.at[k, g, x, fl], r1sem.at[0, k, g], r1sem.at[1, k, g], p).start()
        rx[k, g, x, 0] = hb[k, g, 0, x]

    def r1_done(g, k):
        seven = rd.at[g, pl.ds(0, 7)]
        return remote(seven, seven, r1sem.at[0, k, g], r1sem.at[1, k, g], other)

    def stage_r2(g):
        for k in range(2):
            stage_k(g, k)

    def stage_k(g, k):
        r1_done(g, k).wait_recv()
        rows = rx[k, g].reshape(128, RET)
        rys[k, g] = dot(perm, rows, ((1,), (0,))).astype(BF).reshape(8, 16, RET)
        for j, p in ypeers:
            to = p if k == 0 else across(p)
            remote(rys.at[k, g, j], rd.at[g, k * 8 + y], r2sem.at[0, g], r2sem.at[1, g], to).start()
        if k == 0:
            rd[g, y] = rys[0, g, y]
        else:
            remote(rys.at[1, g, y], rd.at[g, 8 + y], r2sem.at[0, g], r2sem.at[1, g], other).start()

    def r2_done(g):
        fifteen = rd.at[g, pl.ds(0, 15)]
        return remote(fifteen, fifteen, r2sem.at[0, g], r2sem.at[1, g], other)

    def stage_r4(g):
        r2_done(g).wait_recv()
        part = dot(rd[g].reshape(256, RET), gmap[g].reshape(256, 512), ((0,), (0,)))
        oacc[...] = part if g == 0 else oacc[...] + part

    stage_a(0)
    stage_s(0)
    stage_m(0)
    stage_a(1)
    w_remote = remote(w_ref, ww.at[1], wsem.at[1], wsem.at[2], other)
    w_remote.start()
    stage_a(2)
    stage_b(0)
    stage_c(0)
    stage_a(3)
    stage_b(1)
    stage_c(1)
    stage_n(0)
    stage_a(4)
    stage_b(2)
    stage_d(0)
    stage_c(2)
    stage_a(5)
    stage_b(3)
    stage_t(0)
    stage_d(1)
    stage_c(3)
    stage_ab(0)
    stage_m(1)
    stage_b(4)
    stage_ab(1)
    w_local.wait()
    w_remote.wait()
    stage_e(0)
    stage_d(2)
    stage_c(4)
    stage_b(5)
    stage_ab(2)
    stage_bb(0)
    stage_e(1)
    stage_eb(0)
    stage_r1(0)
    stage_d(3)
    stage_c(5)
    stage_bb(1)
    stage_e(2)
    stage_d(4)
    stage_r2(0)
    stage_e(3)
    stage_eb(1)
    stage_r1(1)
    stage_bb(2)
    stage_d(5)
    stage_e(4)
    stage_eb(2)
    stage_r2(1)
    stage_w(5)
    stage_f(5, 0)
    stage_h(2, 0)
    stage_f(5, 1)
    stage_h(2, 1)
    stage_r4(0)
    stage_k(2, 0)
    stage_k(2, 1)
    stage_r4(1)
    stage_r4(2)
    for k in range(2):
        out_ref[k] = oacc[:WIDTH, k * 256 : (k + 1) * 256].astype(BF)

    tok_remote.wait_send()
    ids_remote.wait_send()
    s_done().wait_send()
    pass_copy().wait_send()
    for u in range(len(UNITS)):
        y_done(u).wait_send()
        x_done(u, 0).wait_send()
        x_done(u, 1).wait_send()
        for k in range(8):
            z_copies(u)[0](k).wait_send()
    for g in range(GROUPS):
        yb_done(g).wait_send()
        xb_done(g).wait_send()
        r1_done(g, 0).wait_send()
        r1_done(g, 1).wait_send()
        r2_done(g).wait_send()


def shards(tokens, expert_ids, weights):
    tok = tokens.T
    ids = expert_ids.T
    w = weights.transpose(0, 2, 3, 1).reshape(2 * WIDTH, weights.shape[1])
    units = len(UNITS)
    vmem = pltpu.VMEM
    dma = pltpu.SemaphoreType.DMA
    out = pl.pallas_call(
        kernel,
        out_shape=pltpu.VMEM((2, WIDTH, 256), BF),
        in_specs=[
            pl.BlockSpec(memory_space=pltpu.VMEM),
            pl.BlockSpec(memory_space=pl.ANY),
            pl.BlockSpec(memory_space=pl.ANY),
        ],
        out_specs=pl.BlockSpec(memory_space=pltpu.VMEM),
        scratch_shapes=[
            vmem((HALF, 256), BF),
            vmem((AW, 256), BF),
            vmem((2, 4, 2 * BF_ROWS, 256), BF),
            vmem((2, 256), jnp.int32),
            vmem((2, 2 * WIDTH, 3584), BF),
            vmem((2, GROUPS, 8, 16, AW), BF),
            vmem((2, GROUPS, 8, 16, AW), BF),
            vmem((2, GROUPS, 4, 2, 16, AW), BF),
            vmem((2, GROUPS, 4, 16, AW), BF),
            vmem((2, GROUPS, 4, 2, 4, 16, AW), BF),
            vmem((GROUPS, 8, 16, BW), BF),
            vmem((GROUPS, 8, 16, BW), BF),
            vmem((GROUPS, 4, 2, 16, BW), BF),
            vmem((GROUPS, 4, 2, 16, BW), BF),
            vmem((2, 2 * WIDTH, 128), F32),
            vmem((2, GROUPS, 2, 4, 16, RET), BF),
            vmem((2, GROUPS, 4, 2, 16, RET), BF),
            vmem((2, GROUPS, 8, 16, RET), BF),
            vmem((GROUPS, 16, 16, RET), BF),
            vmem((GROUPS, 2, 128, 512), BF),
            vmem((GROUPS, 128, 512), BF),
            vmem((RET, 512), F32),
            dma((3,)),
            dma((3,)),
            dma((6,)),
            dma((2, units)),
            dma((4, units)),
            dma((8, units)),
            dma((8, units)),
            dma((2, GROUPS)),
            dma((2, GROUPS)),
            dma((2, 2, GROUPS)),
            dma((2, GROUPS)),
        ],
        compiler_params=pltpu.CompilerParams(
            collective_id=1, has_side_effects=True, vmem_limit_bytes=56 << 20
        ),
        cost_estimate=pl.CostEstimate(flops=3355443200, bytes_accessed=5000000, transcendentals=233472),
        name="routed_projections",
    )(ids, tok, w)
    return out.transpose(2, 0, 1)


def solution(mesh):
    return jax.shard_map(
        shards,
        mesh=mesh,
        in_specs=(P("expert", "tensor"), P("expert", None), P("expert", None, None, "tensor")),
        out_specs=P("expert", None, "tensor"),
        check_vma=False,
    )
```

```python
import functools

import jax
import jax.numpy as jnp
from jax import lax
from jax.experimental import pallas as pl
from jax.experimental.pallas import tpu as pltpu
from jax.sharding import PartitionSpec as P

MESH = pl.DeviceIdType.MESH
BF = jnp.bfloat16
F32 = jnp.float32

GROUPS = 3
HALF = 448
AW = 384
BW = 512
BF_ROWS = 64
WIDTH = 304
RET = 384
UNITS = [(0, 0), (0, 1), (1, 0), (1, 1), (2, 0), (2, 1)]


def dot(a, b, dims):
    return lax.dot_general(a, b, (dims, ((), ())), preferred_element_type=F32)


def kernel(
    ids_ref, tok_ref, w_ref, out_ref,
    tokm, toko, tb, ido, ww, ysend, yrecv, xsend, fs, xf, ysb, yrb, xsb, xb,
    acc, hb, rx, rys, rd, gmap, bmap, oacc,
    tsem, wsem, bsem, ysem, xsem, zsend, zrecv, ybsem, xbsem, r1sem, r2sem,
):
    e = lax.axis_index("expert")
    t = lax.axis_index("tensor")
    y = lax.rem(e, 8)
    q = e // 8
    x = q // 2
    zl = lax.rem(q, 2)
    h = t // 2
    c = lax.rem(t, 2)

    def dev(x_, zl_, y_, h_):
        return ((x_ * 2 + zl_) * 8 + y_, h_ * 2 + c)

    def mod4(v):
        return lax.rem(v, 4)

    def across(d):
        return (d[0], d[1] + 1 - 2 * c)

    other = across((e, t))
    zp1 = dev(x, 1 - zl, y, mod4(h + zl))
    zm1 = dev(x, 1 - zl, y, mod4(h + zl + 3))
    zp2 = dev(x, zl, y, mod4(h + 1))
    zm2 = dev(x, zl, y, mod4(h + 3))
    zp3 = dev(x, 1 - zl, y, mod4(h + zl + 1))
    zm3 = dev(x, 1 - zl, y, mod4(h + zl + 2))
    zp4 = dev(x, zl, y, mod4(h + 2))
    line = [zp1, zm1, zp2, zm2, zp3, zm3, zp4]
    ypeers = [(lax.rem(y + d, 8), dev(x, zl, lax.rem(y + d, 8), h)) for d in (4, 3, 5, 2, 6, 1, 7)]
    xpeers = [(mod4(x + d), dev(mod4(x + d), zl, y, h)) for d in (2, 1, 3)]
    qpeers = [
        (mod4(x + d), f, dev(mod4(x + d), (1 - zl) if f else zl, y, h))
        for d, f in ((2, 1), (1, 1), (3, 1), (2, 0), (1, 0), (3, 0), (0, 1))
    ]
    twin = dev(x, 1 - zl, y, h)

    barrier = pltpu.get_barrier_semaphore()
    peers = [p for _, p in ypeers] + [across(p) for _, p in ypeers] + [p for _, _, p in qpeers] + line + [other]
    for p in peers:
        pl.semaphore_signal(barrier, inc=1, device_id=p, device_id_type=MESH)

    def remote(src, dst, ss, rs, p):
        return pltpu.make_async_remote_copy(
            src_ref=src, dst_ref=dst, send_sem=ss, recv_sem=rs, device_id=p, device_id_type=MESH
        )

    tok_local = pltpu.make_async_copy(tok_ref, tokm, tsem.at[0])
    tok_local.start()
    w_local = pltpu.make_async_copy(w_ref, ww.at[0], wsem.at[0])
    w_local.start()

    experts = lax.broadcasted_iota(jnp.int32, (64, 256), 0)
    upper = (
        lax.broadcasted_iota(jnp.int32, (256, 256), 0) < lax.broadcasted_iota(jnp.int32, (256, 256), 1)
    ).astype(F32).astype(BF)

    def slots_of(ids, source_zl):
        counted = jnp.zeros((64, 1), F32)
        slots = []
        for k in range(2):
            expert = ids[k : k + 1, :]
            hot = (experts == expert).astype(F32)
            before = dot(hot.astype(BF), upper, ((1,), (0,))) + counted
            counted = counted + jnp.sum(hot, axis=1, keepdims=True)
            rank = jnp.sum(before * hot, axis=0, keepdims=True).astype(jnp.int32)
            ey, eq = expert & 7, expert >> 3
            flip = (eq + source_zl) & 1
            row = ey * 16 + (eq >> 1) * 4 + flip * 2 + ((rank >> 1) & 1)
            slots.append(((rank & 1) * GROUPS + (rank >> 2)) * 128 + row)
        return slots

    rows_iota = lax.broadcasted_iota(jnp.int32, (128, 256), 0)
    slots = slots_of(ids_ref, zl)

    def build_map(g, k):
        wanted = rows_iota + ((c if k == 0 else 1 - c) * GROUPS + g) * 128
        for choice in range(2):
            gmap[g, k, :, choice * 256 : (choice + 1) * 256] = (slots[choice] == wanted).astype(F32).astype(BF)

    r_out = lax.broadcasted_iota(jnp.int32, (128, 128), 0)
    r_in = lax.broadcasted_iota(jnp.int32, (128, 128), 1)
    perm = (r_in == (r_out & 15) // 2 * 16 + (r_out >> 4) * 2 + (r_out & 1)).astype(F32).astype(BF)

    build_map(0, 0)

    b_rows = pl.ds(pl.multiple_of((1 - c) * AW, 16), BF_ROWS)
    b_dst = pl.ds(pl.multiple_of(c * BF_ROWS, 16), BF_ROWS)
    a_rows = pl.ds(pl.multiple_of(c * BF_ROWS, 16), AW)

    tok_local.wait()
    pl.semaphore_wait(barrier, len(peers))
    tok_remote = remote(tokm.at[a_rows], toko, tsem.at[1], tsem.at[2], other)
    tok_remote.start()
    ids_remote = remote(ids_ref, ido, bsem.at[0], bsem.at[1], twin)
    ids_remote.start()

    def stage_s(_):
        for p in line:
            remote(tokm.at[b_rows], tb.at[zl, h, b_dst], bsem.at[2], bsem.at[3], p).start()
        tb[zl, h, b_dst] = tokm[b_rows]

    def s_done():
        n = BF_ROWS * 7
        return remote(tokm.at[pl.ds(0, n)], tokm.at[pl.ds(0, n)], bsem.at[2], bsem.at[3], other)

    def pass_copy():
        return remote(tb.at[:, :, b_dst], tb.at[:, :, b_dst], bsem.at[4], bsem.at[5], other)

    def stage_t(_):
        s_done().wait_recv()
        pass_copy().start()

    def stage_m(k):
        for g in range(1 - k, GROUPS):
            build_map(g, k)

    def stage_n(_):
        ids_remote.wait_recv()
        theirs = slots_of(ido, 1 - zl)
        flips = (rows_iota >> 1) & 1
        for g in range(GROUPS):
            wanted = rows_iota + (c * GROUPS + g) * 128
            here = (gmap[g, 0, :, :256] + gmap[g, 0, :, 256:]).astype(F32)
            there = jnp.where((theirs[0] == wanted) | (theirs[1] == wanted), 1.0, 0.0)
            bmap[g, :, :256] = jnp.where(flips == 0, here, 0.0).astype(BF)
            bmap[g, :, 256:] = jnp.where(flips == 1, there, 0.0).astype(BF)

    def stage_a(u):
        g, p = UNITS[u]
        dispatch = gmap[g, 0, :, :256] + gmap[g, 0, :, 256:]
        if u == 1:
            remote(toko, toko, tsem.at[1], tsem.at[2], other).wait_recv()
        features = tokm[a_rows] if p == 0 else toko[...]
        ysend[p, g] = dot(dispatch, features, ((1,), (1,))).astype(BF).reshape(8, 16, AW)
        for j, d in ypeers:
            remote(ysend.at[p, g, j], yrecv.at[p, g, y], ysem.at[0, u], ysem.at[1, u], d).start()
        yrecv[p, g, y] = ysend[p, g, y]

    def y_done(u):
        g, p = UNITS[u]
        seven = yrecv.at[p, g, pl.ds(0, 7)]
        return remote(seven, seven, ysem.at[0, u], ysem.at[1, u], other)

    def stage_b(u):
        g, p = UNITS[u]
        y_done(u).wait_recv()
        rows = yrecv[p, g].reshape(128, AW)
        xsend[p, g] = dot(perm, rows, ((1,), (0,))).astype(BF).reshape(4, 2, 16, AW)
        for j, d in xpeers:
            remote(xsend.at[p, g, j, 1], fs.at[p, g, x], xsem.at[2, u], xsem.at[3, u], d).start()
        for j, d in xpeers:
            remote(xsend.at[p, g, j, 0], xf.at[p, g, h, 0, x], xsem.at[0, u], xsem.at[1, u], d).start()
        xf[p, g, h, 0, x] = xsend[p, g, x, 0]
        fs[p, g, x] = xsend[p, g, x, 1]

    def x_done(u, k):
        g, p = UNITS[u]
        three = fs.at[p, g, pl.ds(0, 3)]
        return remote(three, three, xsem.at[2 * k, u], xsem.at[2 * k + 1, u], other)

    def z_copies(u):
        g, p = UNITS[u]

        def near(o):
            return xf.at[p, g, o, 0]

        def half(o, k):
            return xf.at[p, g, o, 0, pl.ds(2 * k, 2)]

        def far(o):
            return xf.at[p, g, o, 1]

        out = [
            (near(h), near(h), zp2), (near(h), near(h), zm2),
            (fs.at[p, g], far(h), zp1), (fs.at[p, g], far(h), zm1),
            (half(mod4(h + 3), 0), half(mod4(h + 3), 0), zp2), (half(mod4(h + 1), 1), half(mod4(h + 1), 1), zm2),
            (far(mod4(h + zl + 3)), far(mod4(h + zl + 3)), zp2), (far(mod4(h + zl)), far(mod4(h + zl)), zm2),
        ]
        inn = [
            near(mod4(h + 3)), near(mod4(h + 1)), far(mod4(h + zl + 3)), far(mod4(h + zl)),
            half(mod4(h + 2), 0), half(mod4(h + 2), 1), far(mod4(h + zl + 2)), far(mod4(h + zl + 1)),
        ]
        return (
            lambda k: remote(out[k][0], out[k][1], zsend.at[k, u], zrecv.at[k, u], out[k][2]),
            lambda k: remote(inn[k], inn[k], zsend.at[k, u], zrecv.at[k, u], other),
        )

    def stage_c(u):
        out, _ = z_copies(u)
        x_done(u, 1).wait_recv()
        out(2).start()
        out(3).start()
        x_done(u, 0).wait_recv()
        out(0).start()
        out(1).start()

    def stage_d(u):
        out, inn = z_copies(u)
        for k, m in ((2, 6), (3, 7), (0, 4), (1, 5)):
            inn(k).wait_recv()
            out(m).start()

    def stage_e(u):
        stage_w(u)
        for k in range(2):
            stage_f(u, k)

    def stage_w(u):
        _, inn = z_copies(u)
        for k in (6, 7, 4, 5):
            inn(k).wait_recv()

    def stage_f(u, k):
        g, p = UNITS[u]
        first = (c if p == 0 else 1 - c) * BW
        total = jnp.zeros((2 * WIDTH, 128), F32) if p == 0 else acc[k]
        for o in range(4):
            cols = pl.ds(pl.multiple_of(o * 2 * HALF + first, 128), AW)
            total = total + dot(ww[k, :, cols], xf[p, g, o].reshape(128, AW), ((1,), (1,)))
        acc[k] = total

    def stage_ab(g):
        if g == 0:
            pass_copy().wait_recv()
        rows = jnp.zeros((128, BW), F32)
        for s, plane in ((0, zl), (1, 1 - zl)):
            features = tb[plane].reshape(BW, 256)
            rows = rows + dot(bmap[g, :, s * 256 : (s + 1) * 256], features, ((1,), (1,)))
        ysb[g] = rows.astype(BF).reshape(8, 16, BW)
        for j, d in ypeers:
            remote(ysb.at[g, j], yrb.at[g, y], ybsem.at[0, g], ybsem.at[1, g], d).start()
        yrb[g, y] = ysb[g, y]

    def yb_done(g):
        seven = yrb.at[g, pl.ds(0, 7)]
        return remote(seven, seven, ybsem.at[0, g], ybsem.at[1, g], other)

    def stage_bb(g):
        yb_done(g).wait_recv()
        rows = yrb[g].reshape(128, BW)
        xsb[g] = dot(perm, rows, ((1,), (0,))).astype(BF).reshape(4, 2, 16, BW)
        for j, d in xpeers:
            remote(xsb.at[g, j], xb.at[g, x], xbsem.at[0, g], xbsem.at[1, g], d).start()
        xb[g, x] = xsb[g, x]

    def xb_done(g):
        three = xb.at[g, pl.ds(0, 3)]
        return remote(three, three, xbsem.at[0, g], xbsem.at[1, g], other)

    def stage_eb(g):
        xb_done(g).wait_recv()
        for k in range(2):
            total = acc[k]
            for o in range(4):
                lanes = slice(o * 128, (o + 1) * 128)
                rows = jnp.concatenate([xb[g, :, f, :, lanes].reshape(64, 128) for f in range(2)])
                cols = slice(o * 2 * HALF + AW, o * 2 * HALF + BW)
                total = total + dot(ww[k, :, cols], rows, ((1,), (1,)))
            acc[k] = total

    def stage_r1(g):
        for k in range(2):
            stage_h(g, k)

    def stage_h(g, k):
        gate, up = acc[k, :WIDTH, :], acc[k, WIDTH:, :]
        value = gate / (1.0 + jnp.exp(-gate)) * up
        value = jnp.concatenate([value, jnp.zeros((RET - WIDTH, 128), F32)])
        hb[k, g] = value.T.astype(BF).reshape(2, 4, 16, RET)
        for j, fl, p in qpeers:
            remote(hb.at[k, g, fl, j], rx.at[k, g, x, fl], r1sem.at[0, k, g], r1sem.at[1, k, g], p).start()
        rx[k, g, x, 0] = hb[k, g, 0, x]

    def r1_done(g, k):
        seven = rd.at[g, pl.ds(0, 7)]
        return remote(seven, seven, r1sem.at[0, k, g], r1sem.at[1, k, g], other)

    def stage_r2(g):
        for k in range(2):
            stage_k(g, k)

    def stage_k(g, k):
        r1_done(g, k).wait_recv()
        rows = rx[k, g].reshape(128, RET)
        rys[k, g] = dot(perm, rows, ((1,), (0,))).astype(BF).reshape(8, 16, RET)
        for j, p in ypeers:
            to = p if k == 0 else across(p)
            remote(rys.at[k, g, j], rd.at[g, k * 8 + y], r2sem.at[0, g], r2sem.at[1, g], to).start()
        if k == 0:
            rd[g, y] = rys[0, g, y]
        else:
            remote(rys.at[1, g, y], rd.at[g, 8 + y], r2sem.at[0, g], r2sem.at[1, g], other).start()

    def r2_done(g):
        fifteen = rd.at[g, pl.ds(0, 15)]
        return remote(fifteen, fifteen, r2sem.at[0, g], r2sem.at[1, g], other)

    def stage_r4(g):
        r2_done(g).wait_recv()
        part = dot(rd[g].reshape(256, RET), gmap[g].reshape(256, 512), ((0,), (0,)))
        oacc[...] = part if g == 0 else oacc[...] + part

    stage_a(0)
    stage_s(0)
    stage_m(0)
    stage_a(1)
    w_remote = remote(w_ref, ww.at[1], wsem.at[1], wsem.at[2], other)
    w_remote.start()
    stage_a(2)
    stage_b(0)
    stage_c(0)
    stage_a(3)
    stage_b(1)
    stage_c(1)
    stage_n(0)
    stage_a(4)
    stage_b(2)
    stage_d(0)
    stage_c(2)
    stage_a(5)
    stage_b(3)
    stage_t(0)
    stage_d(1)
    stage_c(3)
    stage_ab(0)
    stage_m(1)
    stage_b(4)
    w_local.wait()
    w_remote.wait()
    stage_e(0)
    stage_d(2)
    stage_c(4)
    stage_b(5)
    stage_ab(1)
    stage_bb(0)
    stage_e(1)
    stage_eb(0)
    stage_r1(0)
    stage_d(3)
    stage_c(5)
    stage_ab(2)
    stage_bb(1)
    stage_e(2)
    stage_d(4)
    stage_e(3)
    stage_eb(1)
    stage_r1(1)
    stage_r2(0)
    stage_bb(2)
    stage_d(5)
    stage_e(4)
    stage_eb(2)
    stage_r2(1)
    stage_w(5)
    stage_f(5, 0)
    stage_h(2, 0)
    stage_f(5, 1)
    stage_h(2, 1)
    stage_r4(0)
    stage_k(2, 0)
    stage_k(2, 1)
    stage_r4(1)
    stage_r4(2)
    for k in range(2):
        out_ref[k] = oacc[:WIDTH, k * 256 : (k + 1) * 256].astype(BF)

    tok_remote.wait_send()
    ids_remote.wait_send()
    s_done().wait_send()
    pass_copy().wait_send()
    for u in range(len(UNITS)):
        y_done(u).wait_send()
        x_done(u, 0).wait_send()
        x_done(u, 1).wait_send()
        for k in range(8):
            z_copies(u)[0](k).wait_send()
    for g in range(GROUPS):
        yb_done(g).wait_send()
        xb_done(g).wait_send()
        r1_done(g, 0).wait_send()
        r1_done(g, 1).wait_send()
        r2_done(g).wait_send()


def shards(tokens, expert_ids, weights):
    tok = tokens.T
    ids = expert_ids.T
    w = weights.transpose(0, 2, 3, 1).reshape(2 * WIDTH, weights.shape[1])
    units = len(UNITS)
    vmem = pltpu.VMEM
    dma = pltpu.SemaphoreType.DMA
    out = pl.pallas_call(
        kernel,
        out_shape=pltpu.VMEM((2, WIDTH, 256), BF),
        in_specs=[
            pl.BlockSpec(memory_space=pltpu.VMEM),
            pl.BlockSpec(memory_space=pl.ANY),
            pl.BlockSpec(memory_space=pl.ANY),
        ],
        out_specs=pl.BlockSpec(memory_space=pltpu.VMEM),
        scratch_shapes=[
            vmem((HALF, 256), BF),
            vmem((AW, 256), BF),
            vmem((2, 4, 2 * BF_ROWS, 256), BF),
            vmem((2, 256), jnp.int32),
            vmem((2, 2 * WIDTH, 3584), BF),
            vmem((2, GROUPS, 8, 16, AW), BF),
            vmem((2, GROUPS, 8, 16, AW), BF),
            vmem((2, GROUPS, 4, 2, 16, AW), BF),
            vmem((2, GROUPS, 4, 16, AW), BF),
            vmem((2, GROUPS, 4, 2, 4, 16, AW), BF),
            vmem((GROUPS, 8, 16, BW), BF),
            vmem((GROUPS, 8, 16, BW), BF),
            vmem((GROUPS, 4, 2, 16, BW), BF),
            vmem((GROUPS, 4, 2, 16, BW), BF),
            vmem((2, 2 * WIDTH, 128), F32),
            vmem((2, GROUPS, 2, 4, 16, RET), BF),
            vmem((2, GROUPS, 4, 2, 16, RET), BF),
            vmem((2, GROUPS, 8, 16, RET), BF),
            vmem((GROUPS, 16, 16, RET), BF),
            vmem((GROUPS, 2, 128, 512), BF),
            vmem((GROUPS, 128, 512), BF),
            vmem((RET, 512), F32),
            dma((3,)),
            dma((3,)),
            dma((6,)),
            dma((2, units)),
            dma((4, units)),
            dma((8, units)),
            dma((8, units)),
            dma((2, GROUPS)),
            dma((2, GROUPS)),
            dma((2, 2, GROUPS)),
            dma((2, GROUPS)),
        ],
        compiler_params=pltpu.CompilerParams(
            collective_id=1, has_side_effects=True, vmem_limit_bytes=56 << 20
        ),
        cost_estimate=pl.CostEstimate(flops=3355443200, bytes_accessed=5000000, transcendentals=233472),
        name="routed_projections",
    )(ids, tok, w)
    return out.transpose(2, 0, 1)


def solution(mesh):
    return jax.shard_map(
        shards,
        mesh=mesh,
        in_specs=(P("expert", "tensor"), P("expert", None), P("expert", None, None, "tensor")),
        out_specs=P("expert", None, "tensor"),
        check_vma=False,
    )
```
